256 devices in a mesh: node: 32 (over x, y, core), local: 8 (over z).
Axes of the slice: x: 4, y: 4, z: 8, core: 2. Of those that a mesh axis runs over, the one named last changes fastest.
Arguments:
- tokens: bfloat16 [4096, 7168], P('node', 'local'), may hold values from -6 to 6
- w_gate: bfloat16 [32, 7168, 1024], P('node', 'local'), may hold values from -0.0625 to 0.0625
- w_up: bfloat16 [32, 7168, 1024], P('node', 'local'), may hold values from -0.0625 to 0.0625
- w_down: bfloat16 [32, 1024, 7168], P('node', None, 'local'), may hold values from -0.1875 to 0.1875
- expert_ids: int32 [4096, 8], P('node'), may hold values from 0 to 31, all different within a row; in each aligned block of 128 rows (0 to 127, 128 to 255, ...) at most 64 rows name the same one
- gate_weights: bfloat16 [4096, 8], P('node'), may hold values from 0.099609375 to 0.59765625
Outputs:
- moe_out: bfloat16 [4096, 7168], P('node', 'local')
The draws below stay inside these ranges and needn't reach their ends.
Inputs may be any that keep to these rules, and one draw needn't show every extreme that they name: `expert_ids`: each row names 8 different experts. Among the 128 rows of one node no expert is named by more than 64 rows, and in every draw some expert is named by exactly 64 rows of some node.
All inputs are finite; a program needn't handle non-finite values.
Results may differ from the reference program's by a relative error of at most 0.029.
Values may be sent and summed in bfloat16 or wider, within the bound.
A program may use at most 64 MiB of HBM per device.

```python
import math
import jax
import jax.numpy as jnp
import numpy as np
from jax import lax

D = 7168
TOP = 8
H = 1024
TOK_NODE = 128
EXPERTS = 32
CAPN = 64
TOKENS = 4096
N_LOCAL = 8


def block_levels(key, dims, split, least, top_value):
    level, own = 1.0, jax.random.fold_in(key, 6)
    for position, shards_of in split:
        draws = jnp.exp(jax.random.uniform(jax.random.fold_in(own, position), (shards_of,), jnp.float32, least / len(split), top_value / len(split)))
        level = level * jnp.repeat(draws, dims[position] // shards_of).reshape([-1 if axis == position else 1 for axis in range(len(dims))])
    return level


def deal_out(rng, own, number, rows, amount, top, reach, slope):
    sequence = jax.random.permutation(rng, amount)
    heavy_load, usual = shares(amount, rows * top, reach, slope, True), shares(amount, rows * top, reach, slope, False)
    places = jnp.arange(amount)

    def named(sizes, offset_by):
        used = int((sizes > 0).sum())
        fixed = max(1, used // 4)
        passed = fixed + (places - fixed + offset_by * (used - fixed)) % max(1, amount - fixed)
        return jnp.zeros((amount,), jnp.int32).at[sequence[jnp.where(places < fixed, places, passed)]].set(jnp.asarray(sizes, jnp.int32))

    sizes = jnp.where(number % 4 == 0, named(heavy_load, number // 4), named(usual, number - number // 4 - 1))
    mixed = jax.random.permutation(jax.random.fold_in(own, 3), amount)
    source_of, receiver = mixed[0:amount // 2 * 2:2], mixed[1:amount // 2 * 2:2]
    slack = jnp.minimum(sizes[source_of] - 1, reach - sizes[receiver]) // 2
    slack = jnp.where((source_of == sequence[0]) | (receiver == sequence[0]) | (sizes[receiver] == 0), 0, jnp.maximum(slack, 0))
    passed = jax.random.randint(jax.random.fold_in(own, 4), (amount // 2,), 0, 1 << 20) % (slack + 1)
    sizes = sizes.at[source_of].add(-passed).at[receiver].add(passed)
    items = jnp.searchsorted(jnp.cumsum(sizes), jnp.arange(rows * top), side="right").astype(jnp.int32)
    grid = items.reshape(top, rows).T
    grid = grid[jax.random.permutation(jax.random.fold_in(own, 1), rows)]
    offset_by = jax.random.randint(jax.random.fold_in(own, 2), (rows, 1), 0, top)
    return jnp.take_along_axis(grid, (jnp.arange(top)[None, :] + offset_by) % top, axis=1)


def shares(amount, total, reach, slope, full):
    loads = [(1 << 20) // math.isqrt(grade ** slope) + 1 for grade in range(1, amount + 1)]
    largest = reach if full else min(reach, max(-(-total // amount), total * loads[0] // sum(loads)))
    least = 1 if total - largest >= amount - 1 else 0
    counts, surplus = [largest] + [least] * (amount - 1), total - largest - least * (amount - 1)
    while surplus > 0:
        free = [i for i in range(1, amount) if counts[i] < largest] or [i for i in range(1, amount) if counts[i] < reach]
        pool, left = sum([loads[i] for i in free]), surplus
        for i in free:
            addition = min(reach - counts[i], max(1, left * loads[i] // pool), surplus)
            counts[i] = counts[i] + addition
            surplus = surplus - addition
    return np.array(counts)


def gaussian(key, shape, width, most, cuts=(), kind=jnp.bfloat16):
    values = width * jax.random.normal(key, shape, jnp.float32)
    if cuts:
        values = values * block_levels(key, shape, cuts, -0.22, 0.18)
    return jnp.clip(values, -most, most).astype(kind)


def setup_inputs(seed: int = 0) -> dict:
    streams_of = jax.random.split(jax.random.key(seed), 7)
    tokens = gaussian(streams_of[0], (TOKENS, D), 1.0, 6.0, ((0, 32), (1, 8)))
    w_gate = gaussian(streams_of[1], (EXPERTS, D, H), D ** -0.5, 0.0625, ((0, 32), (1, 8)))
    w_up = gaussian(streams_of[2], (EXPERTS, D, H), D ** -0.5, 0.0625, ((0, 32), (1, 8)))
    w_down = gaussian(streams_of[3], (EXPERTS, H, D), H ** -0.5, 0.1875, ((0, 32), (2, 8)))
    expert_ids_keys = jax.random.split(jax.random.fold_in(streams_of[4], 1), TOKENS // TOK_NODE)
    expert_ids_turns = jax.random.permutation(jax.random.fold_in(streams_of[4], 3), TOKENS // TOK_NODE)
    expert_ids = jax.vmap(lambda own, number: deal_out(jax.random.fold_in(streams_of[4], 2), own, number, TOK_NODE, EXPERTS, TOP, CAPN, 2))(expert_ids_keys, expert_ids_turns).reshape((TOKENS, TOP))
    gate_weights = jnp.clip(0.099609375 + 0.49804688 * jax.random.uniform(streams_of[5], (TOKENS, TOP), jnp.float32) ** block_levels(streams_of[5], (TOKENS, TOP), ((0, 32),), -0.2, 0.2), 0.099609375, 0.59765625).astype(jnp.bfloat16)
    return {"tokens": tokens, "w_gate": w_gate, "w_up": w_up, "w_down": w_down, "expert_ids": expert_ids, "gate_weights": gate_weights}


def reference(tokens, w_gate, w_up, w_down, expert_ids, gate_weights):
    total = tokens.shape[0]
    features = D // N_LOCAL
    blocks = tokens.astype(jnp.float32).reshape(total, N_LOCAL, features)
    gate_float = gate_weights.astype(jnp.float32)

    def partial_sum(weights):
        split_weights = weights.astype(jnp.float32).reshape(N_LOCAL, features, H)
        parts = jnp.einsum("tlf,lfh->tlh", blocks, split_weights)
        parts = lax.optimization_barrier(parts.astype(jnp.bfloat16)).astype(jnp.float32)
        return jnp.sum(parts, axis=1)

    def expert_step(expert, running):
        gate = partial_sum(lax.dynamic_index_in_dim(w_gate, expert, 0, False))
        up_sum = partial_sum(lax.dynamic_index_in_dim(w_up, expert, 0, False))
        hidden = (jax.nn.silu(gate) * up_sum).astype(jnp.bfloat16)
        down = lax.dynamic_index_in_dim(w_down, expert, 0, False)
        result = jnp.dot(hidden, down, preferred_element_type=jnp.float32)
        result = lax.optimization_barrier(result.astype(jnp.bfloat16)).astype(jnp.float32)
        weight = jnp.sum(jnp.where(expert_ids == expert, gate_float, jnp.float32(0.0)), axis=1)
        return running + weight[:, None] * result

    summed = lax.fori_loop(0, EXPERTS, expert_step, jnp.zeros((total, D), jnp.float32))
    return summed.astype(jnp.bfloat16)
```

```python
import functools

import jax
import jax.numpy as jnp
from jax import lax
from jax.experimental import pallas as pl
from jax.experimental.pallas import tpu as pltpu
from jax.sharding import PartitionSpec as P

MESH = pl.DeviceIdType.MESH
F32 = jnp.float32
BF16 = jnp.bfloat16

NODES = 32
RING = 8
TOK = 128
FEAT = 896
HID = 1024
HS = HID // RING
CAP = 64
PER = 4
R = PER * CAP
C = NODES // PER
HALF = R // 2


def relative_slot(expert, node):
    dx = (expert // 8 - node // 8) % 4
    dy = ((expert // 2) % 4 - (node // 2) % 4) % 4
    dc = (expert % 2 - node % 2) % 2
    return (dy * 4 + dx) * 2 + dc


def slot_tables(expert_ids, gate_weights):
    node = lax.axis_index("node")
    slots = relative_slot(expert_ids, node).T
    gates = gate_weights.T.astype(F32)
    top = slots.shape[0]
    member = jnp.zeros((NODES, TOK), jnp.int32)
    iota = jnp.arange(NODES, dtype=jnp.int32)
    for k in range(top):
        member = member + (slots[k][None, :] == iota[:, None]).astype(jnp.int32)
    before = jnp.cumsum(member, axis=1) - member
    rows = jnp.arange(NODES * CAP, dtype=jnp.int32)
    select = jnp.zeros((NODES * CAP, TOK), F32)
    combine = jnp.zeros((TOK, NODES * CAP), F32)
    for k in range(top):
        onehot = (slots[k][None, :] == iota[:, None]).astype(jnp.int32)
        placed = slots[k] * CAP + jnp.sum(onehot * before, axis=0)
        select = select + (rows[:, None] == placed[None, :]).astype(F32)
        combine = combine + jnp.where(
            placed[:, None] == rows[None, :], gates[k][:, None], 0.0
        )
    return select.astype(BF16), combine.astype(BF16)


def kernel(
    sel, comb, tok, wg_hbm, wu_hbm, wd_hbm, out,
    wg, wu, wd, outb, arr, snd, rcv, hid, ret, home, acc,
    wsem, dsend, drecv, rsend, rrecv, zsend, zrecv, asend, arecv,
):
    node = lax.axis_index("node")
    z = lax.axis_index("local")
    x, y, core = node // 8, (node // 2) % 4, node % 2
    zup, zdn = (z + 1) % RING, (z + RING - 1) % RING
    neighbour = (zup, zdn)

    weights = [
        pltpu.make_async_copy(src.at[0], dst, wsem.at[k])
        for k, (src, dst) in enumerate(((wg_hbm, wg), (wu_hbm, wu), (wd_hbm, wd)))
    ]
    for copy in weights:
        copy.start()

    def partner(r, sign):
        q = r // 2
        px = (x + sign * (q % 4) + 4) % 4
        py = (y + sign * (q // 4) + 4) % 4
        return (px * 4 + py) * 2 + (core + r) % 2

    barrier = pltpu.get_barrier_semaphore()

    def greet(r, carry):
        pl.semaphore_signal(barrier, inc=1, device_id=(partner(r, 1), z), device_id_type=MESH)
        return carry

    lax.fori_loop(1, NODES, greet, 0)
    for near in neighbour:
        pl.semaphore_signal(barrier, inc=1, device_id=(node, near), device_id_type=MESH)

    def dispatch(r):
        return pltpu.make_async_remote_copy(
            src_ref=outb.at[r], dst_ref=arr.at[r],
            send_sem=dsend.at[r], recv_sem=drecv.at[r],
            device_id=(partner(r, 1), z), device_id_type=MESH,
        )

    def giveback(r):
        return pltpu.make_async_remote_copy(
            src_ref=ret.at[r], dst_ref=home.at[r],
            send_sem=rsend.at[r], recv_sem=rrecv.at[r],
            device_id=(partner(r, -1), z), device_id_type=MESH,
        )

    def partial(i, d, m):
        return pltpu.make_async_remote_copy(
            src_ref=snd.at[i, d, m], dst_ref=rcv.at[i, d, m],
            send_sem=zsend.at[i, d, m], recv_sem=zrecv.at[i, d, m],
            device_id=(node, neighbour[d]), device_id_type=MESH,
        )

    def gather(i, d, a):
        owner = (z + RING - a) % RING if d == 0 else (z + a) % RING
        block = hid.at[i, owner]
        if a == 3:
            block = block.at[pl.ds(d * HALF, HALF)]
        return pltpu.make_async_remote_copy(
            src_ref=block, dst_ref=block,
            send_sem=asend.at[i, d, a], recv_sem=arecv.at[i, d, a],
            device_id=(node, neighbour[d]), device_id_type=MESH,
        )

    def chosen(i):
        rows = sel[pl.ds(pl.multiple_of(i * R, R), R), :]
        return jnp.dot(rows, tok[...], preferred_element_type=F32).astype(BF16)

    first = chosen(0)
    arr[0] = first[:CAP]
    for j in range(1, PER):
        outb[j] = first[j * CAP : (j + 1) * CAP]
    pl.semaphore_wait(barrier, NODES - 1 + 2)
    for j in range(1, PER):
        dispatch(j).start()

    def send_rows(i, carry):
        picked = chosen(i)
        for j in range(PER):
            outb[i * PER + j] = picked[j * CAP : (j + 1) * CAP]
        for j in range(PER):
            dispatch(i * PER + j).start()
        return carry

    lax.fori_loop(1, C, send_rows, 0)
    acc[...] = jnp.zeros_like(acc)
    for copy in weights:
        copy.wait()

    def sums(i, to):
        rows = arr[pl.ds(i * PER, PER)].reshape(R, FEAT)
        cols = pl.ds(pl.multiple_of(to * HS, HS), HS)
        mat = jnp.concatenate([wg[:, cols], wu[:, cols]], axis=1)
        return jnp.dot(rows, mat, preferred_element_type=F32)

    def at(offset):
        return (z + offset + RING) % RING

    def rs_start(i):
        term = sums(i, at(4))
        snd[i, 0, 0] = term[:, :HS].astype(BF16)
        snd[i, 1, 0] = term[:, HS:].astype(BF16)
        partial(i, 0, 0).start()
        partial(i, 1, 0).start()

    def rs_step(i, s):
        terms = (sums(i, at(4 - s)), sums(i, at(s - 4)))
        for part in range(2):
            for d in range(2):
                term = terms[d][:, part * HS : (part + 1) * HS]
                if s == 1:
                    if part == d:
                        partial(i, d, 0).wait_recv()
                        term = term + rcv[i, d, 0].astype(F32)
                else:
                    m = 2 * s - 3 + part
                    partial(i, d, m).wait_recv()
                    term = term + rcv[i, d, m].astype(F32)
                m = 2 * s - 1 + part
                snd[i, d, m] = term.astype(BF16)
                partial(i, d, m).start()

    def finish_sums(i):
        term = sums(i, z)
        total = []
        for part in range(2):
            value = term[:, part * HS : (part + 1) * HS]
            for d in range(2):
                partial(i, d, 5 + part).wait_recv()
                value = value + rcv[i, d, 5 + part].astype(F32)
            total.append(value)
        gate, up = total
        hid[i, z] = (gate / (1.0 + jnp.exp(-gate)) * up).astype(BF16)
        gather(i, 0, 0).start()
        gather(i, 1, 0).start()

    def arrived_block(i, d, a):
        owner = (z + RING - a - 1) % RING if d == 0 else (z + a + 1) % RING
        block = hid.at[i, owner]
        if a == 3:
            block = block.at[pl.ds(d * HALF, HALF)]
        pltpu.make_async_remote_copy(
            src_ref=block, dst_ref=block,
            send_sem=asend.at[i, d, a], recv_sem=arecv.at[i, d, a],
            device_id=(node, neighbour[d]), device_id_type=MESH,
        ).wait_recv()

    def ag_step(i, a):
        for d in range(2):
            arrived_block(i, d, a - 1)
            gather(i, d, a).start()

    def down(i):
        for d in range(2):
            arrived_block(i, d, 3)
        hidden = jnp.concatenate([hid[i, k] for k in range(RING)], axis=1)
        result = jnp.dot(hidden, wd[...], preferred_element_type=F32).astype(BF16)
        for j in range(PER):
            ret[i * PER + j] = result[j * CAP : (j + 1) * CAP]

        @pl.when(i == 0)
        def _():
            home[0] = result[:CAP]

        @pl.when(i > 0)
        def _():
            giveback(i * PER).start()

        for j in range(1, PER):
            giveback(i * PER + j).start()

    def combine(i):
        @pl.when(i > 0)
        def _():
            giveback(i * PER).wait_recv()

        for j in range(1, PER):
            giveback(i * PER + j).wait_recv()
        rows = home[pl.ds(i * PER, PER)].reshape(R, FEAT)
        weight = comb[:, pl.ds(pl.multiple_of(i * R, R), R)]
        acc[...] += jnp.dot(weight, rows, preferred_element_type=F32)

    def step(i, carry):
        @pl.when(i < C)
        def _():
            @pl.when(i > 0)
            def _():
                dispatch(i * PER).wait_recv()

            for j in range(1, PER):
                dispatch(i * PER + j).wait_recv()
            rs_start(i)

        @pl.when((i >= 1) & (i <= C))
        def _():
            finish_sums(i - 1)

        @pl.when((i >= 2) & (i <= C + 1))
        def _():
            down(i - 2)

        for s in range(1, 4):
            @pl.when(i < C)
            def _():
                rs_step(i, s)

            @pl.when((i >= 1) & (i <= C))
            def _():
                ag_step(i - 1, s)

        @pl.when((i >= 4) & (i <= C + 3))
        def _():
            combine(i - 4)

        return carry

    lax.fori_loop(0, C + 4, step, 0)
    out[...] = acc[...].astype(BF16)

    def drain_nodes(r, carry):
        dispatch(r).wait_send()
        giveback(r).wait_send()
        return carry

    lax.fori_loop(1, NODES, drain_nodes, 0)

    def drain_ring(i, carry):
        for d in range(2):
            for m in range(7):
                partial(i, d, m).wait_send()
            for a in range(4):
                gather(i, d, a).wait_send()
        return carry

    lax.fori_loop(0, C, drain_ring, 0)


def per_device(tokens, w_gate, w_up, w_down, expert_ids, gate_weights):
    select, combine = slot_tables(expert_ids, gate_weights)
    vmem = pl.BlockSpec(memory_space=pltpu.VMEM)
    hbm = pl.BlockSpec(memory_space=pl.ANY)
    dma = pltpu.SemaphoreType.DMA
    return pl.pallas_call(
        kernel,
        out_shape=jax.ShapeDtypeStruct((TOK, FEAT), BF16),
        in_specs=[vmem, vmem, vmem, hbm, hbm, hbm],
        out_specs=vmem,
        scratch_shapes=[
            pltpu.VMEM((FEAT, HID), BF16),
            pltpu.VMEM((FEAT, HID), BF16),
            pltpu.VMEM((HID, FEAT), BF16),
            pltpu.VMEM((NODES, CAP, FEAT), BF16),
            pltpu.VMEM((NODES, CAP, FEAT), BF16),
            pltpu.VMEM((C, 2, 7, R, HS), BF16),
            pltpu.VMEM((C, 2, 7, R, HS), BF16),
            pltpu.VMEM((C, RING, R, HS), BF16),
            pltpu.VMEM((NODES, CAP, FEAT), BF16),
            pltpu.VMEM((NODES, CAP, FEAT), BF16),
            pltpu.VMEM((TOK, FEAT), F32),
            dma((3,)),
            dma((NODES,)), dma((NODES,)),
            dma((NODES,)), dma((NODES,)),
            dma((C, 2, 7)), dma((C, 2, 7)),
            dma((C, 2, 4)), dma((C, 2, 4)),
        ],
        compiler_params=pltpu.CompilerParams(
            collective_id=0, has_side_effects=True, vmem_limit_bytes=56 * 2**20
        ),
    )(select, combine, tokens, w_gate, w_up, w_down)


def solution(mesh):
    placed = (
        P("node", "local"),
        P("node", "local", None),
        P("node", "local", None),
        P("node", None, "local"),
        P("node", None),
        P("node", None),
    )
    return jax.shard_map(
        per_device, mesh=mesh, in_specs=placed, out_specs=P("node", "local"), check_vma=False
    )
```

```python
import functools

import jax
import jax.numpy as jnp
from jax import lax
from jax.experimental import pallas as pl
from jax.experimental.pallas import tpu as pltpu
from jax.sharding import PartitionSpec as P

MESH = pl.DeviceIdType.MESH
F32 = jnp.float32
BF16 = jnp.bfloat16

NODES = 32
RING = 8
TOK = 128
FEAT = 896
HID = 1024
HS = HID // RING
CAP = 64

SLOTS = (
    (0, 0, 0), (0, 0, 1),
    (1, 0, 1), (3, 0, 1), (0, 1, 0), (0, 3, 0),
    (0, 1, 1), (0, 3, 1), (2, 0, 0), (2, 0, 1),
    (1, 1, 0), (3, 3, 0), (1, 3, 0), (3, 1, 0),
    (2, 1, 0), (2, 3, 0), (1, 2, 0), (3, 2, 0),
    (0, 2, 0), (0, 2, 1), (2, 2, 0), (2, 2, 1),
    (2, 1, 1), (2, 3, 1), (1, 2, 1), (3, 2, 1),
    (1, 1, 1), (3, 3, 1), (1, 3, 1), (3, 1, 1),
    (1, 0, 0), (3, 0, 0),
)
FULL, PART = 4, 2
C = 2 + (NODES - 2 * PART) // FULL
R = FULL * CAP


def lookup(index, values):
    found = 0
    for k, value in enumerate(values):
        found = found + jnp.where(index == k, value, 0)
    return found


def kernel(
    ids, gates, tok_hbm, wg_hbm, wu_hbm, wd_hbm, out,
    tok, wg, wu, wd, key, dense, outb, arr, snd, rcv, hid, ret, home, acc,
    wsem, dsend, drecv, rsend, rrecv, zsend, zrecv, asend, arecv,
):
    node = lax.axis_index("node")
    z = lax.axis_index("local")
    x, y, core = node // 8, (node // 2) % 4, node % 2
    neighbour = ((z + 1) % RING, (z + RING - 1) % RING)

    pairs = ((tok_hbm, tok), (wg_hbm.at[0], wg), (wu_hbm.at[0], wu), (wd_hbm.at[0], wd))
    loads = [pltpu.make_async_copy(src, dst, wsem.at[k]) for k, (src, dst) in enumerate(pairs)]
    for copy in loads:
        copy.start()

    def partner(r, sign):
        px = (x + sign * lookup(r, [dx for dx, _, _ in SLOTS]) + 4) % 4
        py = (y + sign * lookup(r, [dy for _, dy, _ in SLOTS]) + 4) % 4
        return (px * 4 + py) * 2 + (core + lookup(r, [dc for _, _, dc in SLOTS])) % 2

    barrier = pltpu.get_barrier_semaphore()

    def greet(r, carry):
        pl.semaphore_signal(barrier, inc=1, device_id=(partner(r, 1), z), device_id_type=MESH)
        return carry

    for near in neighbour:
        pl.semaphore_signal(barrier, inc=1, device_id=(node, near), device_id_type=MESH)
    lax.fori_loop(1, NODES, greet, 0)

    expert = ids[...]
    dx = ((expert >> 3) - x) & 3
    dy = (((expert >> 1) & 3) - y) & 3
    dc = ((expert & 1) - core) & 1
    order = [SLOTS.index((k // 8, (k // 2) % 4, k % 2)) for k in range(NODES)]
    slot = lookup(dx * 8 + dy * 2 + dc, order)
    weight = gates[...].astype(F32)
    iota = lax.broadcasted_iota(jnp.int32, (NODES, TOK), 0)
    member = jnp.zeros((NODES, TOK), F32)
    spread = jnp.zeros((NODES, TOK), F32)
    for k in range(ids.shape[0]):
        match = iota == slot[k : k + 1, :]
        member = member + jnp.where(match, 1.0, 0.0)
        spread = spread + jnp.where(match, weight[k : k + 1, :], 0.0)
    lower = lax.broadcasted_iota(jnp.int32, (TOK, TOK), 0) < lax.broadcasted_iota(
        jnp.int32, (TOK, TOK), 1
    )
    before = jnp.dot(
        member.astype(BF16), jnp.where(lower, 1.0, 0.0).astype(BF16), preferred_element_type=F32
    )
    key[...] = jnp.where(member > 0.0, before, -1.0)
    dense[...] = spread

    def base(i):
        return jnp.maximum(FULL * i - (FULL - PART), 0)

    def dispatch(r):
        return pltpu.make_async_remote_copy(
            src_ref=outb.at[r], dst_ref=arr.at[r],
            send_sem=dsend.at[r], recv_sem=drecv.at[r],
            device_id=(partner(r, 1), z), device_id_type=MESH,
        )

    def giveback(r):
        return pltpu.make_async_remote_copy(
            src_ref=ret.at[r], dst_ref=home.at[r],
            send_sem=rsend.at[r], recv_sem=rrecv.at[r],
            device_id=(partner(r, -1), z), device_id_type=MESH,
        )

    def others(i, n, act):
        for j in range(n):
            if j == 0 and n == PART:
                pl.when(i > 0)(functools.partial(act, base(i), 0))
            else:
                act(base(i) + j, j)

    def partial(i, n, d, m):
        rows = pl.ds(0, n * CAP)
        return pltpu.make_async_remote_copy(
            src_ref=snd.at[i, d, m, rows], dst_ref=rcv.at[i, d, m, rows],
            send_sem=zsend.at[i, d, m], recv_sem=zrecv.at[i, d, m],
            device_id=(node, neighbour[d]), device_id_type=MESH,
        )

    def gather(i, n, d, a, back=0):
        far = a + back
        owner = (z + RING - far) % RING if d == 0 else (z + far) % RING
        half = n * CAP // 2
        rows = pl.ds(d * half, half) if a == 3 else pl.ds(0, n * CAP)
        block = hid.at[i, owner, rows]
        return pltpu.make_async_remote_copy(
            src_ref=block, dst_ref=block,
            send_sem=asend.at[i, d, a], recv_sem=arecv.at[i, d, a],
            device_id=(node, neighbour[d]), device_id_type=MESH,
        )

    place = lax.broadcasted_iota(jnp.int32, (CAP, TOK), 0).astype(F32)

    def select(i, n):
        return [place == key[pl.ds(base(i) + j, 1), :] for j in range(n)]

    def pick(i, n):
        onehot = jnp.concatenate([jnp.where(s, 1.0, 0.0) for s in select(i, n)], axis=0)
        rows = jnp.dot(onehot.astype(BF16), tok[...], preferred_element_type=F32).astype(BF16)

        def keep(r, j):
            outb[r] = rows[j * CAP : (j + 1) * CAP]

        others(i, n, keep)
        return rows

    def send_rows(i, n):
        others(i, n, lambda r, j: dispatch(r).start())

    loads[0].wait()
    arr[0] = pick(0, PART)[:CAP]
    pick(1, FULL)
    pl.semaphore_wait(barrier, NODES - 1 + 2)
    send_rows(0, PART)
    send_rows(1, FULL)
    acc[...] = jnp.zeros_like(acc)
    for copy in loads[1:]:
        copy.wait()

    def sums(i, n, to):
        rows = arr[pl.ds(base(i), n)].reshape(n * CAP, FEAT)
        cols = pl.ds(pl.multiple_of(to * HS, HS), HS)
        mat = jnp.concatenate([wg[:, cols], wu[:, cols]], axis=1)
        return jnp.dot(rows, mat, preferred_element_type=F32)

    def at(offset):
        return (z + offset + RING) % RING

    def rs_start(i, n):
        others(i, n, lambda r, j: dispatch(r).wait_recv())
        term = sums(i, n, at(4))
        for d in range(2):
            snd[i, d, 0, : n * CAP] = term[:, d * HS : (d + 1) * HS].astype(BF16)
            partial(i, n, d, 0).start()

    def rs_step(i, n, s):
        terms = (sums(i, n, at(4 - s)), sums(i, n, at(s - 4)))
        for part in range(2):
            for d in range(2):
                term = terms[d][:, part * HS : (part + 1) * HS]
                if s > 1 or part == d:
                    m = 0 if s == 1 else 2 * s - 3 + part
                    partial(i, n, d, m).wait_recv()
                    term = term + rcv[i, d, m, : n * CAP].astype(F32)
                m = 2 * s - 1 + part
                snd[i, d, m, : n * CAP] = term.astype(BF16)
                partial(i, n, d, m).start()

    def finish_sums(i, n):
        term = sums(i, n, z)
        total = []
        for part in range(2):
            value = term[:, part * HS : (part + 1) * HS]
            for d in range(2):
                partial(i, n, d, 5 + part).wait_recv()
                value = value + rcv[i, d, 5 + part, : n * CAP].astype(F32)
            total.append(value)
        gate, up = total
        hid[i, z, : n * CAP] = (gate / (1.0 + jnp.exp(-gate)) * up).astype(BF16)
        for d in range(2):
            gather(i, n, d, 0).start()

    def ag_step(i, n, a):
        for d in range(2):
            gather(i, n, d, a - 1, back=1).wait_recv()
            gather(i, n, d, a).start()

    def down(i, n):
        for d in range(2):
            gather(i, n, d, 3, back=1).wait_recv()
        hidden = jnp.concatenate([hid[i, k, : n * CAP] for k in range(RING)], axis=1)
        result = jnp.dot(hidden, wd[...], preferred_element_type=F32).astype(BF16)

        def send(r, j):
            ret[r] = result[j * CAP : (j + 1) * CAP]
            giveback(r).start()

        others(i, n, send)
        if n == PART:
            @pl.when(i == 0)
            def _():
                home[0] = result[:CAP]

    def combine(i, n):
        others(i, n, lambda r, j: giveback(r).wait_recv())
        rows = home[pl.ds(base(i), n)].reshape(n * CAP, FEAT)
        mix = jnp.concatenate(
            [
                jnp.where(s, dense[pl.ds(base(i) + j, 1), :], 0.0)
                for j, s in enumerate(select(i, n))
            ],
            axis=0,
        )
        acc[...] += lax.dot_general(
            mix.astype(BF16), rows, (((0,), (0,)), ((), ())), preferred_element_type=F32
        )

    def prepare(i, n):
        pick(i, n)
        send_rows(i, n)

    def step(i, carry):
        def live(k, act, *more):
            pl.when((i == k) | (i == C - 1 + k))(lambda: act(i - k, PART, *more))
            pl.when((i > k) & (i < C - 1 + k))(lambda: act(i - k, FULL, *more))

        live(0, rs_start)
        live(1, rs_step, 2)
        live(2, finish_sums)
        live(3, ag_step, 2)
        pl.when(i < C - 3)(lambda: prepare(i + 2, FULL))
        pl.when(i == C - 3)(lambda: prepare(i + 2, PART))
        live(4, down)
        live(0, rs_step, 1)
        live(1, rs_step, 3)
        live(2, ag_step, 1)
        live(3, ag_step, 3)
        live(6, combine)
        return carry

    lax.fori_loop(0, C + 6, step, 0)
    out[...] = acc[...].astype(BF16)

    def drain_nodes(r, carry):
        dispatch(r).wait_send()
        giveback(r).wait_send()
        return carry

    lax.fori_loop(1, NODES, drain_nodes, 0)

    def drain_ring(i, n):
        for d in range(2):
            for m in range(7):
                partial(i, n, d, m).wait_send()
            for a in range(4):
                gather(i, n, d, a).wait_send()

    drain_ring(0, PART)
    drain_ring(C - 1, PART)

    def drain_full(i, carry):
        drain_ring(i, FULL)
        return carry

    lax.fori_loop(1, C - 1, drain_full, 0)


def per_device(tokens, w_gate, w_up, w_down, expert_ids, gate_weights):
    vmem = pl.BlockSpec(memory_space=pltpu.VMEM)
    hbm = pl.BlockSpec(memory_space=pl.ANY)
    dma = pltpu.SemaphoreType.DMA
    return pl.pallas_call(
        kernel,
        out_shape=jax.ShapeDtypeStruct((TOK, FEAT), BF16),
        in_specs=[vmem, vmem, hbm, hbm, hbm, hbm],
        out_specs=vmem,
        scratch_shapes=[
            pltpu.VMEM((TOK, FEAT), BF16),
            pltpu.VMEM((FEAT, HID), BF16),
            pltpu.VMEM((FEAT, HID), BF16),
            pltpu.VMEM((HID, FEAT), BF16),
            pltpu.VMEM((NODES, TOK), F32),
            pltpu.VMEM((NODES, TOK), F32),
            pltpu.VMEM((NODES, CAP, FEAT), BF16),
            pltpu.VMEM((NODES, CAP, FEAT), BF16),
            pltpu.VMEM((C, 2, 7, R, HS), BF16),
            pltpu.VMEM((C, 2, 7, R, HS), BF16),
            pltpu.VMEM((C, RING, R, HS), BF16),
            pltpu.VMEM((NODES, CAP, FEAT), BF16),
            pltpu.VMEM((NODES, CAP, FEAT), BF16),
            pltpu.VMEM((TOK, FEAT), F32),
            dma((4,)),
            dma((NODES,)), dma((NODES,)),
            dma((NODES,)), dma((NODES,)),
            dma((C, 2, 7)), dma((C, 2, 7)),
            dma((C, 2, 4)), dma((C, 2, 4)),
        ],
        compiler_params=pltpu.CompilerParams(
            collective_id=0, has_side_effects=True, vmem_limit_bytes=58 * 2**20
        ),
    )(expert_ids.T, gate_weights.T, tokens, w_gate, w_up, w_down)


def solution(mesh):
    placed = (
        P("node", "local"),
        P("node", "local", None),
        P("node", "local", None),
        P("node", None, "local"),
        P("node", None),
        P("node", None),
    )
    return jax.shard_map(
        per_device, mesh=mesh, in_specs=placed, out_specs=P("node", "local"), check_vma=False
    )
```

```python
import functools

import jax
import jax.numpy as jnp
from jax import lax
from jax.experimental import pallas as pl
from jax.experimental.pallas import tpu as pltpu
from jax.sharding import PartitionSpec as P

MESH = pl.DeviceIdType.MESH
F32 = jnp.float32
BF16 = jnp.bfloat16

NODES = 32
RING = 8
TOK = 128
FEAT = 896
HID = 1024
HS = HID // RING
CAP = 64

SLOTS = (
    (0, 0, 0), (0, 0, 1),
    (1, 0, 1), (3, 0, 1), (0, 1, 0), (0, 3, 0),
    (1, 1, 0), (3, 3, 0), (1, 3, 0), (3, 1, 0),
    (2, 1, 0), (2, 3, 0), (1, 2, 0), (3, 2, 0),
    (0, 2, 0), (0, 2, 1), (2, 2, 0), (2, 2, 1),
    (2, 1, 1), (2, 3, 1), (1, 2, 1), (3, 2, 1),
    (1, 1, 1), (3, 3, 1), (1, 3, 1), (3, 1, 1),
    (0, 1, 1), (0, 3, 1), (2, 0, 0), (2, 0, 1),
    (1, 0, 0), (3, 0, 0),
)
FULL, PART = 4, 2
C = 2 + (NODES - 2 * PART) // FULL
R = FULL * CAP


def lookup(index, values):
    found = 0
    for k, value in enumerate(values):
        found = found + jnp.where(index == k, value, 0)
    return found


def kernel(
    ids, gates, tok_hbm, wg_hbm, wu_hbm, wd_hbm, out,
    tok, wg, wu, wd, key, dense, outb, arr, snd, rcv, hid, ret, home, acc,
    wsem, dsend, drecv, rsend, rrecv, zsend, zrecv, asend, arecv,
):
    node = lax.axis_index("node")
    z = lax.axis_index("local")
    x, y, core = node // 8, (node // 2) % 4, node % 2
    neighbour = ((z + 1) % RING, (z + RING - 1) % RING)

    pairs = ((tok_hbm, tok), (wg_hbm.at[0], wg), (wu_hbm.at[0], wu), (wd_hbm.at[0], wd))
    loads = [pltpu.make_async_copy(src, dst, wsem.at[k]) for k, (src, dst) in enumerate(pairs)]
    for copy in loads:
        copy.start()

    def shifted(dx, dy, dc, sign):
        return (((x + sign * dx + 4) % 4) * 4 + (y + sign * dy + 4) % 4) * 2 + (core + dc) % 2

    def partner(i, n, j, sign):
        if n == PART:
            chunks, index = (0, C - 1), jnp.where(i == 0, 0, 1)
        else:
            chunks, index = range(1, C - 1), i - 1
        offsets = [SLOTS[max(FULL * k - (FULL - PART), 0) + j] for k in chunks]
        return shifted(*(lookup(index, [o[axis] for o in offsets]) for axis in range(3)), sign)

    barrier = pltpu.get_barrier_semaphore()

    for near in neighbour:
        pl.semaphore_signal(barrier, inc=1, device_id=(node, near), device_id_type=MESH)
    for offset in SLOTS[1:]:
        other = shifted(*offset, 1)
        pl.semaphore_signal(barrier, inc=1, device_id=(other, z), device_id_type=MESH)

    expert = ids[...]
    dx = ((expert >> 3) - x) & 3
    dy = (((expert >> 1) & 3) - y) & 3
    dc = ((expert & 1) - core) & 1
    order = [SLOTS.index((k // 8, (k // 2) % 4, k % 2)) for k in range(NODES)]
    slot = lookup(dx * 8 + dy * 2 + dc, order)
    weight = gates[...].astype(F32)
    iota = lax.broadcasted_iota(jnp.int32, (NODES, TOK), 0)
    member = jnp.zeros((NODES, TOK), F32)
    spread = jnp.zeros((NODES, TOK), F32)
    for k in range(ids.shape[0]):
        match = iota == slot[k : k + 1, :]
        member = member + jnp.where(match, 1.0, 0.0)
        spread = spread + jnp.where(match, weight[k : k + 1, :], 0.0)
    lower = lax.broadcasted_iota(jnp.int32, (TOK, TOK), 0) < lax.broadcasted_iota(
        jnp.int32, (TOK, TOK), 1
    )
    before = jnp.dot(
        member.astype(BF16), jnp.where(lower, 1.0, 0.0).astype(BF16), preferred_element_type=F32
    )
    key[...] = jnp.where(member > 0.0, before, -1.0)
    dense[...] = spread

    def base(i):
        return jnp.maximum(FULL * i - (FULL - PART), 0)

    def dispatch(i, n, j):
        r = base(i) + j
        return pltpu.make_async_remote_copy(
            src_ref=outb.at[r], dst_ref=arr.at[r],
            send_sem=dsend.at[r], recv_sem=drecv.at[r],
            device_id=(partner(i, n, j, 1), z), device_id_type=MESH,
        )

    def giveback(i, n, j):
        r = base(i) + j
        return pltpu.make_async_remote_copy(
            src_ref=ret.at[r], dst_ref=home.at[r],
            send_sem=rsend.at[r], recv_sem=rrecv.at[r],
            device_id=(partner(i, n, j, -1), z), device_id_type=MESH,
        )

    def others(i, n, act):
        for j in range(n):
            if j == 0 and n == PART:
                pl.when(i > 0)(functools.partial(act, 0))
            else:
                act(j)

    def partial(i, n, d, m):
        rows = pl.ds(0, n * CAP)
        return pltpu.make_async_remote_copy(
            src_ref=snd.at[i, d, m, rows], dst_ref=rcv.at[i, d, m, rows],
            send_sem=zsend.at[i, d, m], recv_sem=zrecv.at[i, d, m],
            device_id=(node, neighbour[d]), device_id_type=MESH,
        )

    def gather(i, n, d, a, back=0):
        far = a + back
        owner = (z + RING - far) % RING if d == 0 else (z + far) % RING
        half = n * CAP // 2
        rows = pl.ds(d * half, half) if a == 3 else pl.ds(0, n * CAP)
        block = hid.at[i, owner, rows]
        return pltpu.make_async_remote_copy(
            src_ref=block, dst_ref=block,
            send_sem=asend.at[i, d, a], recv_sem=arecv.at[i, d, a],
            device_id=(node, neighbour[d]), device_id_type=MESH,
        )

    place = lax.broadcasted_iota(jnp.int32, (CAP, TOK), 0).astype(F32)

    def select(i, n):
        return [place == key[pl.ds(base(i) + j, 1), :] for j in range(n)]

    def pick(i, n):
        onehot = jnp.concatenate([jnp.where(s, 1.0, 0.0) for s in select(i, n)], axis=0)
        rows = jnp.dot(onehot.astype(BF16), tok[...], preferred_element_type=F32).astype(BF16)

        def keep(j):
            outb[base(i) + j] = rows[j * CAP : (j + 1) * CAP]

        others(i, n, keep)
        return rows

    def send_rows(i, n):
        others(i, n, lambda j: dispatch(i, n, j).start())

    loads[0].wait()
    arr[0] = pick(0, PART)[:CAP]
    pick(1, FULL)
    pl.semaphore_wait(barrier, NODES - 1 + 2)
    send_rows(0, PART)
    send_rows(1, FULL)
    acc[...] = jnp.zeros_like(acc)
    for copy in loads[1:]:
        copy.wait()

    def sums(i, n, to):
        rows = arr[pl.ds(base(i), n)].reshape(n * CAP, FEAT)
        cols = pl.ds(pl.multiple_of(to * HS, HS), HS)
        mat = jnp.concatenate([wg[:, cols], wu[:, cols]], axis=1)
        return jnp.dot(rows, mat, preferred_element_type=F32)

    def at(offset):
        return (z + offset + RING) % RING

    def rs_start(i, n):
        others(i, n, lambda j: dispatch(i, n, j).wait_recv())
        term = sums(i, n, at(4))
        for d in range(2):
            snd[i, d, 0, : n * CAP] = term[:, d * HS : (d + 1) * HS].astype(BF16)
            partial(i, n, d, 0).start()

    def rs_step(i, n, s):
        terms = (sums(i, n, at(4 - s)), sums(i, n, at(s - 4)))
        for part in range(2):
            for d in range(2):
                term = terms[d][:, part * HS : (part + 1) * HS]
                if s > 1 or part == d:
                    m = 0 if s == 1 else 2 * s - 3 + part
                    partial(i, n, d, m).wait_recv()
                    term = term + rcv[i, d, m, : n * CAP].astype(F32)
                m = 2 * s - 1 + part
                snd[i, d, m, : n * CAP] = term.astype(BF16)
                partial(i, n, d, m).start()

    def finish_sums(i, n):
        term = sums(i, n, z)
        total = []
        for part in range(2):
            value = term[:, part * HS : (part + 1) * HS]
            for d in range(2):
                partial(i, n, d, 5 + part).wait_recv()
                value = value + rcv[i, d, 5 + part, : n * CAP].astype(F32)
            total.append(value)
        gate, up = total
        hid[i, z, : n * CAP] = (gate / (1.0 + jnp.exp(-gate)) * up).astype(BF16)
        for d in range(2):
            gather(i, n, d, 0).start()

    def ag_step(i, n, a):
        for d in range(2):
            gather(i, n, d, a - 1, back=1).wait_recv()
            gather(i, n, d, a).start()

    def down(i, n):
        for d in range(2):
            gather(i, n, d, 3, back=1).wait_recv()
        hidden = jnp.concatenate([hid[i, k, : n * CAP] for k in range(RING)], axis=1)
        result = jnp.dot(hidden, wd[...], preferred_element_type=F32).astype(BF16)

        def send(j):
            ret[base(i) + j] = result[j * CAP : (j + 1) * CAP]
            giveback(i, n, j).start()

        others(i, n, send)
        if n == PART:
            @pl.when(i == 0)
            def _():
                home[0] = result[:CAP]

        others(i, n, lambda j: dispatch(i, n, j).wait_send())
        for d in range(2):
            for m in range(7):
                partial(i, n, d, m).wait_send()
            for a in range(4):
                gather(i, n, d, a).wait_send()

    def combine(i, n):
        others(i, n, lambda j: giveback(i, n, j).wait_recv())
        rows = home[pl.ds(base(i), n)].reshape(n * CAP, FEAT)
        mix = jnp.concatenate(
            [
                jnp.where(s, dense[pl.ds(base(i) + j, 1), :], 0.0)
                for j, s in enumerate(select(i, n))
            ],
            axis=0,
        )
        acc[...] += lax.dot_general(
            mix.astype(BF16), rows, (((0,), (0,)), ((), ())), preferred_element_type=F32
        )
        others(i, n, lambda j: giveback(i, n, j).wait_send())

    def prepare(i, n):
        pick(i, n)
        send_rows(i, n)

    def step(i, carry):
        def live(k, act, *more):
            pl.when((i == k) | (i == C - 1 + k))(lambda: act(i - k, PART, *more))
            pl.when((i > k) & (i < C - 1 + k))(lambda: act(i - k, FULL, *more))

        live(0, rs_start)
        live(1, rs_step, 2)
        live(2, finish_sums)
        live(3, ag_step, 2)
        live(4, down)
        live(0, rs_step, 1)
        live(1, rs_step, 3)
        live(2, ag_step, 1)
        live(3, ag_step, 3)
        pl.when(i < C - 3)(lambda: prepare(i + 2, FULL))
        pl.when(i == C - 3)(lambda: prepare(i + 2, PART))
        live(6, combine)
        return carry

    lax.fori_loop(0, C + 6, step, 0)
    out[...] = acc[...].astype(BF16)


def per_device(tokens, w_gate, w_up, w_down, expert_ids, gate_weights):
    vmem = pl.BlockSpec(memory_space=pltpu.VMEM)
    hbm = pl.BlockSpec(memory_space=pl.ANY)
    dma = pltpu.SemaphoreType.DMA
    return pl.pallas_call(
        kernel,
        out_shape=jax.ShapeDtypeStruct((TOK, FEAT), BF16),
        in_specs=[vmem, vmem, hbm, hbm, hbm, hbm],
        out_specs=vmem,
        scratch_shapes=[
            pltpu.VMEM((TOK, FEAT), BF16),
            pltpu.VMEM((FEAT, HID), BF16),
            pltpu.VMEM((FEAT, HID), BF16),
            pltpu.VMEM((HID, FEAT), BF16),
            pltpu.VMEM((NODES, TOK), F32),
            pltpu.VMEM((NODES, TOK), F32),
            pltpu.VMEM((NODES, CAP, FEAT), BF16),
            pltpu.VMEM((NODES, CAP, FEAT), BF16),
            pltpu.VMEM((C, 2, 7, R, HS), BF16),
            pltpu.VMEM((C, 2, 7, R, HS), BF16),
            pltpu.VMEM((C, RING, R, HS), BF16),
            pltpu.VMEM((NODES, CAP, FEAT), BF16),
            pltpu.VMEM((NODES, CAP, FEAT), BF16),
            pltpu.VMEM((TOK, FEAT), F32),
            dma((4,)),
            dma((NODES,)), dma((NODES,)),
            dma((NODES,)), dma((NODES,)),
            dma((C, 2, 7)), dma((C, 2, 7)),
            dma((C, 2, 4)), dma((C, 2, 4)),
        ],
        compiler_params=pltpu.CompilerParams(
            collective_id=0, has_side_effects=True, vmem_limit_bytes=58 * 2**20
        ),
    )(expert_ids.T, gate_weights.T, tokens, w_gate, w_up, w_down)


def solution(mesh):
    placed = (
        P("node", "local"),
        P("node", "local", None),
        P("node", "local", None),
        P("node", None, "local"),
        P("node", None),
        P("node", None),
    )
    return jax.shard_map(
        per_device, mesh=mesh, in_specs=placed, out_specs=P("node", "local"), check_vma=False
    )
```

```python
import functools

import jax
import jax.numpy as jnp
from jax import lax
from jax.experimental import pallas as pl
from jax.experimental.pallas import tpu as pltpu
from jax.sharding import PartitionSpec as P

MESH = pl.DeviceIdType.MESH
F32 = jnp.float32
BF16 = jnp.bfloat16

NODES = 32
RING = 8
TOK = 128
FEAT = 896
HID = 1024
HS = HID // RING
CAP = 64

SLOTS = (
    (0, 0, 0), (0, 0, 1),
    (1, 0, 1), (3, 0, 1), (0, 1, 0), (0, 3, 0),
    (1, 1, 0), (3, 3, 0), (1, 3, 0), (3, 1, 0),
    (2, 2, 0), (2, 2, 1), (0, 1, 1), (0, 3, 1),
    (2, 1, 0), (2, 3, 0), (1, 2, 0), (3, 2, 0),
    (2, 1, 1), (2, 3, 1), (1, 2, 1), (3, 2, 1),
    (1, 1, 1), (3, 3, 1), (1, 3, 1), (3, 1, 1),
    (2, 0, 0), (2, 0, 1), (0, 2, 0), (0, 2, 1),
    (1, 0, 0), (3, 0, 0),
)
FULL, PART = 4, 2
C = 2 + (NODES - 2 * PART) // FULL
R = FULL * CAP


def lookup(index, values):
    found = 0
    for k, value in enumerate(values):
        found = found + jnp.where(index == k, value, 0)
    return found


def kernel(
    ids, gates, tok_hbm, wg_hbm, wu_hbm, wd_hbm, out,
    tok, wg, wu, wd, key, dense, outb, arr, snd, rcv, hid, ret, home, acc,
    wsem, dsend, drecv, rsend, rrecv, zsend, zrecv, asend, arecv,
):
    node = lax.axis_index("node")
    z = lax.axis_index("local")
    x, y, core = node // 8, (node // 2) % 4, node % 2
    neighbour = ((z + 1) % RING, (z + RING - 1) % RING)

    pairs = ((tok_hbm, tok), (wg_hbm.at[0], wg), (wu_hbm.at[0], wu), (wd_hbm.at[0], wd))
    loads = [pltpu.make_async_copy(src, dst, wsem.at[k]) for k, (src, dst) in enumerate(pairs)]
    for copy in loads:
        copy.start()

    def shifted(dx, dy, dc, sign):
        return (((x + sign * dx + 4) % 4) * 4 + (y + sign * dy + 4) % 4) * 2 + (core + dc) % 2

    def partner(i, n, j, sign):
        if n == PART:
            chunks, index = (0, C - 1), jnp.where(i == 0, 0, 1)
        else:
            chunks, index = range(1, C - 1), i - 1
        offsets = [SLOTS[max(FULL * k - (FULL - PART), 0) + j] for k in chunks]
        return shifted(*(lookup(index, [o[axis] for o in offsets]) for axis in range(3)), sign)

    barrier = pltpu.get_barrier_semaphore()

    for near in neighbour:
        pl.semaphore_signal(barrier, inc=1, device_id=(node, near), device_id_type=MESH)
    for offset in SLOTS[1:]:
        other = shifted(*offset, 1)
        pl.semaphore_signal(barrier, inc=1, device_id=(other, z), device_id_type=MESH)

    expert = ids[...]
    dx = ((expert >> 3) - x) & 3
    dy = (((expert >> 1) & 3) - y) & 3
    dc = ((expert & 1) - core) & 1
    order = [SLOTS.index((k // 8, (k // 2) % 4, k % 2)) for k in range(NODES)]
    slot = lookup(dx * 8 + dy * 2 + dc, order)
    weight = gates[...].astype(F32)
    iota = lax.broadcasted_iota(jnp.int32, (NODES, TOK), 0)
    member = jnp.zeros((NODES, TOK), F32)
    spread = jnp.zeros((NODES, TOK), F32)
    for k in range(ids.shape[0]):
        match = iota == slot[k : k + 1, :]
        member = member + jnp.where(match, 1.0, 0.0)
        spread = spread + jnp.where(match, weight[k : k + 1, :], 0.0)
    lower = lax.broadcasted_iota(jnp.int32, (TOK, TOK), 0) < lax.broadcasted_iota(
        jnp.int32, (TOK, TOK), 1
    )
    before = jnp.dot(
        member.astype(BF16), jnp.where(lower, 1.0, 0.0).astype(BF16), preferred_element_type=F32
    )
    key[...] = jnp.where(member > 0.0, before, -1.0)
    dense[...] = spread

    def base(i):
        return jnp.maximum(FULL * i - (FULL - PART), 0)

    def dispatch(i, n, j):
        r = base(i) + j
        return pltpu.make_async_remote_copy(
            src_ref=outb.at[r], dst_ref=arr.at[r],
            send_sem=dsend.at[r], recv_sem=drecv.at[r],
            device_id=(partner(i, n, j, 1), z), device_id_type=MESH,
        )

    def giveback(i, n, j):
        r = base(i) + j
        return pltpu.make_async_remote_copy(
            src_ref=ret.at[r], dst_ref=home.at[r],
            send_sem=rsend.at[r], recv_sem=rrecv.at[r],
            device_id=(partner(i, n, j, -1), z), device_id_type=MESH,
        )

    def others(i, n, act):
        for j in range(n):
            if j == 0 and n == PART:
                pl.when(i > 0)(functools.partial(act, 0))
            else:
                act(j)

    def partial(i, n, d, m):
        rows = pl.ds(0, n * CAP)
        return pltpu.make_async_remote_copy(
            src_ref=snd.at[i, d, m, rows], dst_ref=rcv.at[i, d, m, rows],
            send_sem=zsend.at[i, d, m], recv_sem=zrecv.at[i, d, m],
            device_id=(node, neighbour[d]), device_id_type=MESH,
        )

    def gather(i, n, d, a, back=0):
        far = a + back
        owner = (z + RING - far) % RING if d == 0 else (z + far) % RING
        half = n * CAP // 2
        rows = pl.ds(d * half, half) if a == 3 else pl.ds(0, n * CAP)
        block = hid.at[i, owner, rows]
        return pltpu.make_async_remote_copy(
            src_ref=block, dst_ref=block,
            send_sem=asend.at[i, d, a], recv_sem=arecv.at[i, d, a],
            device_id=(node, neighbour[d]), device_id_type=MESH,
        )

    place = lax.broadcasted_iota(jnp.int32, (CAP, TOK), 0).astype(F32)

    def select(i, n):
        return [place == key[pl.ds(base(i) + j, 1), :] for j in range(n)]

    def pick(i, n):
        onehot = jnp.concatenate([jnp.where(s, 1.0, 0.0) for s in select(i, n)], axis=0)
        rows = jnp.dot(onehot.astype(BF16), tok[...], preferred_element_type=F32).astype(BF16)

        def keep(j):
            outb[base(i) + j] = rows[j * CAP : (j + 1) * CAP]

        others(i, n, keep)
        return rows

    def send_rows(i, n):
        others(i, n, lambda j: dispatch(i, n, j).start())

    loads[0].wait()
    arr[0] = pick(0, PART)[:CAP]
    pick(1, FULL)
    pl.semaphore_wait(barrier, NODES - 1 + 2)
    send_rows(0, PART)
    send_rows(1, FULL)
    acc[...] = jnp.zeros_like(acc)
    for copy in loads[1:]:
        copy.wait()

    def sums(i, n, to):
        rows = arr[pl.ds(base(i), n)].reshape(n * CAP, FEAT)
        cols = pl.ds(pl.multiple_of(to * HS, HS), HS)
        mat = jnp.concatenate([wg[:, cols], wu[:, cols]], axis=1)
        return jnp.dot(rows, mat, preferred_element_type=F32)

    def at(offset):
        return (z + offset + RING) % RING

    def rs_start(i, n):
        others(i, n, lambda j: dispatch(i, n, j).wait_recv())
        term = sums(i, n, at(4))
        for d in range(2):
            snd[i, d, 0, : n * CAP] = term[:, d * HS : (d + 1) * HS].astype(BF16)
            partial(i, n, d, 0).start()

    def rs_step(i, n, s):
        terms = (sums(i, n, at(4 - s)), sums(i, n, at(s - 4)))
        for part in range(2):
            for d in range(2):
                term = terms[d][:, part * HS : (part + 1) * HS]
                if s > 1 or part == d:
                    m = 0 if s == 1 else 2 * s - 3 + part
                    partial(i, n, d, m).wait_recv()
                    term = term + rcv[i, d, m, : n * CAP].astype(F32)
                m = 2 * s - 1 + part
                snd[i, d, m, : n * CAP] = term.astype(BF16)
                partial(i, n, d, m).start()

    def finish_sums(i, n):
        term = sums(i, n, z)
        total = []
        for part in range(2):
            value = term[:, part * HS : (part + 1) * HS]
            for d in range(2):
                partial(i, n, d, 5 + part).wait_recv()
                value = value + rcv[i, d, 5 + part, : n * CAP].astype(F32)
            total.append(value)
        gate, up = total
        hid[i, z, : n * CAP] = (gate / (1.0 + jnp.exp(-gate)) * up).astype(BF16)
        for d in range(2):
            gather(i, n, d, 0).start()

    def ag_step(i, n, a):
        for d in range(2):
            gather(i, n, d, a - 1, back=1).wait_recv()
            gather(i, n, d, a).start()

    def down(i, n):
        for d in range(2):
            gather(i, n, d, 3, back=1).wait_recv()
        hidden = jnp.concatenate([hid[i, k, : n * CAP] for k in range(RING)], axis=1)
        result = jnp.dot(hidden, wd[...], preferred_element_type=F32).astype(BF16)

        def send(j):
            ret[base(i) + j] = result[j * CAP : (j + 1) * CAP]
            giveback(i, n, j).start()

        others(i, n, send)
        if n == PART:
            @pl.when(i == 0)
            def _():
                home[0] = result[:CAP]

    def combine(i, n):
        mix = jnp.concatenate(
            [
                jnp.where(s, dense[pl.ds(base(i) + j, 1), :], 0.0)
                for j, s in enumerate(select(i, n))
            ],
            axis=0,
        ).astype(BF16)
        others(i, n, lambda j: dispatch(i, n, j).wait_send())
        for d in range(2):
            for m in range(7):
                partial(i, n, d, m).wait_send()
            for a in range(4):
                gather(i, n, d, a).wait_send()
        others(i, n, lambda j: giveback(i, n, j).wait_recv())
        rows = home[pl.ds(base(i), n)].reshape(n * CAP, FEAT)
        acc[...] += lax.dot_general(
            mix, rows, (((0,), (0,)), ((), ())), preferred_element_type=F32
        )
        others(i, n, lambda j: giveback(i, n, j).wait_send())

    def prepare(i, n):
        pick(i, n)
        send_rows(i, n)

    def step(i, carry):
        def live(k, act, *more):
            pl.when((i == k) | (i == C - 1 + k))(lambda: act(i - k, PART, *more))
            pl.when((i > k) & (i < C - 1 + k))(lambda: act(i - k, FULL, *more))

        live(0, rs_start)
        live(1, rs_step, 2)
        live(2, finish_sums)
        live(3, ag_step, 2)
        live(4, down)
        live(0, rs_step, 1)
        live(1, rs_step, 3)
        live(2, ag_step, 1)
        live(3, ag_step, 3)
        pl.when(i < C - 3)(lambda: prepare(i + 2, FULL))
        pl.when(i == C - 3)(lambda: prepare(i + 2, PART))
        live(6, combine)
        return carry

    lax.fori_loop(0, C + 6, step, 0)
    out[...] = acc[...].astype(BF16)


def per_device(tokens, w_gate, w_up, w_down, expert_ids, gate_weights):
    vmem = pl.BlockSpec(memory_space=pltpu.VMEM)
    hbm = pl.BlockSpec(memory_space=pl.ANY)
    dma = pltpu.SemaphoreType.DMA
    return pl.pallas_call(
        kernel,
        out_shape=jax.ShapeDtypeStruct((TOK, FEAT), BF16),
        in_specs=[vmem, vmem, hbm, hbm, hbm, hbm],
        out_specs=vmem,
        scratch_shapes=[
            pltpu.VMEM((TOK, FEAT), BF16),
            pltpu.VMEM((FEAT, HID), BF16),
            pltpu.VMEM((FEAT, HID), BF16),
            pltpu.VMEM((HID, FEAT), BF16),
            pltpu.VMEM((NODES, TOK), F32),
            pltpu.VMEM((NODES, TOK), F32),
            pltpu.VMEM((NODES, CAP, FEAT), BF16),
            pltpu.VMEM((NODES, CAP, FEAT), BF16),
            pltpu.VMEM((C, 2, 7, R, HS), BF16),
            pltpu.VMEM((C, 2, 7, R, HS), BF16),
            pltpu.VMEM((C, RING, R, HS), BF16),
            pltpu.VMEM((NODES, CAP, FEAT), BF16),
            pltpu.VMEM((NODES, CAP, FEAT), BF16),
            pltpu.VMEM((TOK, FEAT), F32),
            dma((4,)),
            dma((NODES,)), dma((NODES,)),
            dma((NODES,)), dma((NODES,)),
            dma((C, 2, 7)), dma((C, 2, 7)),
            dma((C, 2, 4)), dma((C, 2, 4)),
        ],
        compiler_params=pltpu.CompilerParams(
            collective_id=0, has_side_effects=True, vmem_limit_bytes=58 * 2**20
        ),
    )(expert_ids.T, gate_weights.T, tokens, w_gate, w_up, w_down)


def solution(mesh):
    placed = (
        P("node", "local"),
        P("node", "local", None),
        P("node", "local", None),
        P("node", None, "local"),
        P("node", None),
        P("node", None),
    )
    return jax.shard_map(
        per_device, mesh=mesh, in_specs=placed, out_specs=P("node", "local"), check_vma=False
    )
```

```python
import functools

import jax
import jax.numpy as jnp
from jax import lax
from jax.experimental import pallas as pl
from jax.experimental.pallas import tpu as pltpu
from jax.sharding import PartitionSpec as P

MESH = pl.DeviceIdType.MESH
F32 = jnp.float32
BF16 = jnp.bfloat16

NODES = 32
RING = 8
TOK = 128
FEAT = 896
HID = 1024
HS = HID // RING
CAP = 64

SLOTS = (
    (0, 0, 0), (0, 0, 1),
    (1, 0, 1), (3, 0, 1), (0, 1, 0), (0, 3, 0),
    (1, 1, 0), (3, 3, 0), (1, 3, 0), (3, 1, 0),
    (2, 2, 0), (2, 2, 1), (0, 1, 1), (0, 3, 1),
    (2, 1, 0), (2, 3, 0), (1, 2, 0), (3, 2, 0),
    (2, 1, 1), (2, 3, 1), (1, 2, 1), (3, 2, 1),
    (1, 1, 1), (3, 3, 1), (1, 3, 1), (3, 1, 1),
    (2, 0, 0), (2, 0, 1), (0, 2, 0), (0, 2, 1),
    (1, 0, 0), (3, 0, 0),
)
FULL, PART = 4, 2
C = 2 + (NODES - 2 * PART) // FULL
R = FULL * CAP


def lookup(index, values):
    found = 0
    for k, value in enumerate(values):
        found = found + jnp.where(index == k, value, 0)
    return found


def kernel(
    ids, gates, tok_hbm, wg_hbm, wu_hbm, wd_hbm, out,
    tok, wg, wu, wd, key, dense, outb, arr, snd, rcv, hid, ret, home, acc,
    wsem, dsend, drecv, rsend, rrecv, zsend, zrecv, asend, arecv,
):
    node = lax.axis_index("node")
    z = lax.axis_index("local")
    x, y, core = node // 8, (node // 2) % 4, node % 2
    turn = 1 - 2 * core

    def at(offset):
        return (z + turn * offset + RING) % RING

    neighbour = (at(1), at(-1))

    pairs = ((tok_hbm, tok), (wg_hbm.at[0], wg), (wu_hbm.at[0], wu), (wd_hbm.at[0], wd))
    loads = [pltpu.make_async_copy(src, dst, wsem.at[k]) for k, (src, dst) in enumerate(pairs)]
    for copy in loads:
        copy.start()

    def shifted(dx, dy, dc, sign):
        return (((x + sign * dx + 4) % 4) * 4 + (y + sign * dy + 4) % 4) * 2 + (core + dc) % 2

    def partner(i, n, j, sign):
        if n == PART:
            chunks, index = (0, C - 1), jnp.where(i == 0, 0, 1)
        else:
            chunks, index = range(1, C - 1), i - 1
        offsets = [SLOTS[max(FULL * k - (FULL - PART), 0) + j] for k in chunks]
        return shifted(*(lookup(index, [o[axis] for o in offsets]) for axis in range(3)), sign)

    barrier = pltpu.get_barrier_semaphore()

    for near in neighbour:
        pl.semaphore_signal(barrier, inc=1, device_id=(node, near), device_id_type=MESH)
    for offset in SLOTS[1:]:
        other = shifted(*offset, 1)
        pl.semaphore_signal(barrier, inc=1, device_id=(other, z), device_id_type=MESH)

    expert = ids[...]
    dx = ((expert >> 3) - x) & 3
    dy = (((expert >> 1) & 3) - y) & 3
    dc = ((expert & 1) - core) & 1
    order = [SLOTS.index((k // 8, (k // 2) % 4, k % 2)) for k in range(NODES)]
    slot = lookup(dx * 8 + dy * 2 + dc, order)
    weight = gates[...].astype(F32)
    iota = lax.broadcasted_iota(jnp.int32, (NODES, TOK), 0)
    member = jnp.zeros((NODES, TOK), F32)
    spread = jnp.zeros((NODES, TOK), F32)
    for k in range(ids.shape[0]):
        match = iota == slot[k : k + 1, :]
        member = member + jnp.where(match, 1.0, 0.0)
        spread = spread + jnp.where(match, weight[k : k + 1, :], 0.0)
    lower = lax.broadcasted_iota(jnp.int32, (TOK, TOK), 0) < lax.broadcasted_iota(
        jnp.int32, (TOK, TOK), 1
    )
    before = jnp.dot(
        member.astype(BF16), jnp.where(lower, 1.0, 0.0).astype(BF16), preferred_element_type=F32
    )
    key[...] = jnp.where(member > 0.0, before, -1.0)
    dense[...] = spread

    def base(i):
        return jnp.maximum(FULL * i - (FULL - PART), 0)

    def dispatch(i, n, j):
        r = base(i) + j
        return pltpu.make_async_remote_copy(
            src_ref=outb.at[r], dst_ref=arr.at[r],
            send_sem=dsend.at[r], recv_sem=drecv.at[r],
            device_id=(partner(i, n, j, 1), z), device_id_type=MESH,
        )

    def giveback(i, n, j):
        r = base(i) + j
        return pltpu.make_async_remote_copy(
            src_ref=ret.at[r], dst_ref=home.at[r],
            send_sem=rsend.at[r], recv_sem=rrecv.at[r],
            device_id=(partner(i, n, j, -1), z), device_id_type=MESH,
        )

    def others(i, n, act):
        for j in range(n):
            if j == 0 and n == PART:
                pl.when(i > 0)(functools.partial(act, 0))
            else:
                act(j)

    def partial(i, n, d, m):
        rows = pl.ds(0, n * CAP)
        return pltpu.make_async_remote_copy(
            src_ref=snd.at[i, d, m, rows], dst_ref=rcv.at[i, d, m, rows],
            send_sem=zsend.at[i, d, m], recv_sem=zrecv.at[i, d, m],
            device_id=(node, neighbour[d]), device_id_type=MESH,
        )

    def gather(i, n, d, a, back=0):
        far = a + back
        owner = at(-far if d == 0 else far)
        half = n * CAP // 2
        rows = pl.ds(d * half, half) if a == 3 else pl.ds(0, n * CAP)
        block = hid.at[i, owner, rows]
        return pltpu.make_async_remote_copy(
            src_ref=block, dst_ref=block,
            send_sem=asend.at[i, d, a], recv_sem=arecv.at[i, d, a],
            device_id=(node, neighbour[d]), device_id_type=MESH,
        )

    place = lax.broadcasted_iota(jnp.int32, (CAP, TOK), 0).astype(F32)

    def select(i, n):
        return [place == key[pl.ds(base(i) + j, 1), :] for j in range(n)]

    def pick(i, n):
        onehot = jnp.concatenate([jnp.where(s, 1.0, 0.0) for s in select(i, n)], axis=0)
        rows = jnp.dot(onehot.astype(BF16), tok[...], preferred_element_type=F32).astype(BF16)

        def keep(j):
            outb[base(i) + j] = rows[j * CAP : (j + 1) * CAP]

        others(i, n, keep)
        return rows

    def send_rows(i, n):
        others(i, n, lambda j: dispatch(i, n, j).start())

    loads[0].wait()
    arr[0] = pick(0, PART)[:CAP]
    pick(1, FULL)
    pl.semaphore_wait(barrier, NODES - 1 + 2)
    send_rows(0, PART)
    send_rows(1, FULL)
    acc[...] = jnp.zeros_like(acc)
    for copy in loads[1:]:
        copy.wait()

    def sums(i, n, to):
        rows = arr[pl.ds(base(i), n)].reshape(n * CAP, FEAT)
        cols = pl.ds(pl.multiple_of(to * HS, HS), HS)
        mat = jnp.concatenate([wg[:, cols], wu[:, cols]], axis=1)
        return jnp.dot(rows, mat, preferred_element_type=F32)

    def rs_start(i, n):
        others(i, n, lambda j: dispatch(i, n, j).wait_recv())
        term = sums(i, n, at(4))
        for d in range(2):
            snd[i, d, 0, : n * CAP] = term[:, d * HS : (d + 1) * HS].astype(BF16)
            partial(i, n, d, 0).start()

    def rs_step(i, n, s):
        terms = (sums(i, n, at(4 - s)), sums(i, n, at(s - 4)))
        for part in range(2):
            for d in range(2):
                term = terms[d][:, part * HS : (part + 1) * HS]
                if s > 1 or part == d:
                    m = 0 if s == 1 else 2 * s - 3 + part
                    partial(i, n, d, m).wait_recv()
                    term = term + rcv[i, d, m, : n * CAP].astype(F32)
                m = 2 * s - 1 + part
                snd[i, d, m, : n * CAP] = term.astype(BF16)
                partial(i, n, d, m).start()

    def finish_sums(i, n):
        term = sums(i, n, z)
        total = []
        for part in range(2):
            value = term[:, part * HS : (part + 1) * HS]
            for d in range(2):
                partial(i, n, d, 5 + part).wait_recv()
                value = value + rcv[i, d, 5 + part, : n * CAP].astype(F32)
            total.append(value)
        gate, up = total
        hid[i, z, : n * CAP] = (gate / (1.0 + jnp.exp(-gate)) * up).astype(BF16)
        for d in range(2):
            gather(i, n, d, 0).start()

    def ag_step(i, n, a):
        for d in range(2):
            gather(i, n, d, a - 1, back=1).wait_recv()
            gather(i, n, d, a).start()

    def down(i, n):
        def product(offsets):
            owners = [at(o) for o in offsets]
            hidden = jnp.concatenate([hid[i, k, : n * CAP] for k in owners], axis=1)
            rows = [wd[pl.ds(pl.multiple_of(k * HS, HS), HS), :] for k in owners]
            return jnp.dot(hidden, jnp.concatenate(rows, axis=0), preferred_element_type=F32)

        near = product((0, 1, -1, 2, -2, 3, -3))
        for d in range(2):
            gather(i, n, d, 3, back=1).wait_recv()
        result = (near + product((4,))).astype(BF16)

        def send(j):
            ret[base(i) + j] = result[j * CAP : (j + 1) * CAP]
            giveback(i, n, j).start()

        others(i, n, send)
        if n == PART:
            @pl.when(i == 0)
            def _():
                home[0] = result[:CAP]

    def combine(i, n):
        mix = jnp.concatenate(
            [
                jnp.where(s, dense[pl.ds(base(i) + j, 1), :], 0.0)
                for j, s in enumerate(select(i, n))
            ],
            axis=0,
        ).astype(BF16)
        others(i, n, lambda j: dispatch(i, n, j).wait_send())
        for d in range(2):
            for m in range(7):
                partial(i, n, d, m).wait_send()
            for a in range(4):
                gather(i, n, d, a).wait_send()
        others(i, n, lambda j: giveback(i, n, j).wait_recv())
        rows = home[pl.ds(base(i), n)].reshape(n * CAP, FEAT)
        acc[...] += lax.dot_general(
            mix, rows, (((0,), (0,)), ((), ())), preferred_element_type=F32
        )
        others(i, n, lambda j: giveback(i, n, j).wait_send())

    def prepare(i, n):
        pick(i, n)
        send_rows(i, n)

    def step(i, carry):
        def live(k, act, *more):
            pl.when((i == k) | (i == C - 1 + k))(lambda: act(i - k, PART, *more))
            pl.when((i > k) & (i < C - 1 + k))(lambda: act(i - k, FULL, *more))

        live(0, rs_start)
        live(1, rs_step, 2)
        live(2, finish_sums)
        live(3, ag_step, 2)
        live(4, down)
        live(0, rs_step, 1)
        live(1, rs_step, 3)
        live(2, ag_step, 1)
        live(3, ag_step, 3)
        pl.when(i < C - 3)(lambda: prepare(i + 2, FULL))
        pl.when(i == C - 3)(lambda: prepare(i + 2, PART))
        live(6, combine)
        return carry

    lax.fori_loop(0, C + 6, step, 0)
    out[...] = acc[...].astype(BF16)


def per_device(tokens, w_gate, w_up, w_down, expert_ids, gate_weights):
    vmem = pl.BlockSpec(memory_space=pltpu.VMEM)
    hbm = pl.BlockSpec(memory_space=pl.ANY)
    dma = pltpu.SemaphoreType.DMA
    return pl.pallas_call(
        kernel,
        out_shape=jax.ShapeDtypeStruct((TOK, FEAT), BF16),
        in_specs=[vmem, vmem, hbm, hbm, hbm, hbm],
        out_specs=vmem,
        scratch_shapes=[
            pltpu.VMEM((TOK, FEAT), BF16),
            pltpu.VMEM((FEAT, HID), BF16),
            pltpu.VMEM((FEAT, HID), BF16),
            pltpu.VMEM((HID, FEAT), BF16),
            pltpu.VMEM((NODES, TOK), F32),
            pltpu.VMEM((NODES, TOK), F32),
            pltpu.VMEM((NODES, CAP, FEAT), BF16),
            pltpu.VMEM((NODES, CAP, FEAT), BF16),
            pltpu.VMEM((C, 2, 7, R, HS), BF16),
            pltpu.VMEM((C, 2, 7, R, HS), BF16),
            pltpu.VMEM((C, RING, R, HS), BF16),
            pltpu.VMEM((NODES, CAP, FEAT), BF16),
            pltpu.VMEM((NODES, CAP, FEAT), BF16),
            pltpu.VMEM((TOK, FEAT), F32),
            dma((4,)),
            dma((NODES,)), dma((NODES,)),
            dma((NODES,)), dma((NODES,)),
            dma((C, 2, 7)), dma((C, 2, 7)),
            dma((C, 2, 4)), dma((C, 2, 4)),
        ],
        compiler_params=pltpu.CompilerParams(
            collective_id=0, has_side_effects=True, vmem_limit_bytes=58 * 2**20
        ),
    )(expert_ids.T, gate_weights.T, tokens, w_gate, w_up, w_down)


def solution(mesh):
    placed = (
        P("node", "local"),
        P("node", "local", None),
        P("node", "local", None),
        P("node", None, "local"),
        P("node", None),
        P("node", None),
    )
    return jax.shard_map(
        per_device, mesh=mesh, in_specs=placed, out_specs=P("node", "local"), check_vma=False
    )
```
